128 devices in a mesh: scene: 32 (over x, z, core), tie: 4 (over y).
Axes of the slice: x: 4, y: 4, z: 4, core: 2. Of those that a mesh axis runs over, the one named last changes fastest.
Arguments:
- tie_rows: bfloat16 [384, 256, 256], P('tie'), may hold values from -0.375 to 0.375
- point_counts: int32 [384], P('tie'), may hold values from 1 to 128, as said below
- pattern: int32 [512, 384], P('scene', 'tie'), may hold values 0 or 1
- sensitivity: bfloat16 [512, 192, 192], P('scene'), may hold values from -0.119628906 to 0.119628906
- damping: float32 [512], P(('scene', 'tie')), may hold values from 1 to 8
- prior: float32 [64], replicated, may hold values from 0.25 to 4
Outputs:
- scene_rows: float32 [512, 192, 256], P(('scene', 'tie'))
- global_factor: float32 [64, 64], replicated
The draws below stay inside these ranges and needn't reach their ends.
Inputs may be any that keep to these rules, and one draw needn't show every extreme that they name: `point_counts`: points present in each block; some block is full.
All inputs are finite; a program needn't handle non-finite values. No bound on the sum of `pattern` on one device may be relied on, other than what follows from the above.
Results may differ from the reference program's by a relative error of at most 0.0003.
Values sent between devices are 32-bit elements; how exact they have to be, the bound alone decides.
No kernel may reach another device: no remote copies, remote signals or barrier semaphores. Data moves between devices by JAX's collectives and lax.ppermute only.
A program may use at most 128 MiB of HBM per device.

```python
import math
import jax
import jax.numpy as jnp
from jax import lax

SPLINE = 192
SHARED = 64
COLS = 256
PTS = 128
ROWS = 256
SC_SHARD = 16
NSC = 512
NBLK = 384
N_SCENE = 32


def draw_point_counts(key, part):
    first_key, second_key = jax.random.split(jax.random.fold_in(key, 11))
    counts = jax.random.randint(first_key, (NBLK,), PTS // 4, PTS + 1)
    chosen = jax.random.randint(second_key, (), 0, NBLK)
    return jnp.where(jnp.arange(NBLK) == chosen, PTS, counts).astype(jnp.int32)


def plant(drawn, key, smallest, top_value):
    spot = [jax.random.randint(jax.random.fold_in(key, axis), (), 0, length) for axis, length in enumerate(drawn.shape)]
    main_axis = drawn.shape.index(max(drawn.shape))
    neighbour = spot[:main_axis] + [(spot[main_axis] + 1) % drawn.shape[main_axis]] + spot[main_axis + 1:]
    return drawn.at[tuple(spot)].set(smallest).at[tuple(neighbour)].set(top_value)


def block_levels(stream_key, extent, pieces, least, largest):
    def one(axis_at, shards_of):
        heights = jax.random.uniform(jax.random.fold_in(jax.random.fold_in(stream_key, 6), axis_at), (shards_of,), jnp.float32, least / len(pieces), largest / len(pieces))
        return jnp.repeat(jnp.exp(heights), extent[axis_at] // shards_of).reshape((-1,) + (1,) * (len(extent) - axis_at - 1))

    gain = one(*pieces[0])
    for cut in pieces[1:]:
        gain = gain * one(*cut)
    return gain


def normal_values(rng, dims, spread, most, pieces=(), kind=jnp.bfloat16):
    result = spread * jax.random.normal(rng, dims, jnp.float32)
    if pieces:
        result = result * block_levels(rng, dims, pieces, -0.22, 0.18)
    return jnp.clip(result, -most, most).astype(kind)


def setup_inputs(seed: int = 0) -> dict:
    key_list = jax.random.split(jax.random.key(seed), 7)
    return {
        "tie_rows": normal_values(key_list[0], (NBLK, ROWS, COLS), ROWS ** -0.5, 0.375, ((0, 4),)),
        "point_counts": draw_point_counts(jax.random.fold_in(key_list[6], 71), 0),
        "pattern": plant((jax.random.randint(key_list[2], (NSC, NBLK), 0, 16) < 1).astype(jnp.int32), jax.random.fold_in(key_list[2], 1), 0, 1),
        "sensitivity": normal_values(key_list[3], (NSC, SPLINE, SPLINE), 0.02, 0.119628906, ((0, 32),)),
        "damping": jnp.clip(jnp.exp(math.log(8.0) - 2.0794415 * jax.random.uniform(key_list[4], (NSC,), jnp.float32) ** block_levels(key_list[4], (NSC,), ((0, 128),), -0.2, 0.2)), 1.0, 8.0),
        "prior": jnp.clip(jnp.exp(jax.random.uniform(key_list[5], (SHARED,), jnp.float32, math.log(0.25), math.log(4.0))), 0.25, 4.0),
    }


highest = lax.Precision.HIGHEST

def block_gram(tie_rows, point_counts):
    row_index = lax.broadcasted_iota(jnp.int32, (tie_rows.shape[0], tie_rows.shape[1]), 1)
    row_valid = (row_index // 2 < point_counts[:, None]).astype(jnp.float32)
    full_rows = tie_rows.astype(jnp.float32)
    masked_rows = full_rows * row_valid[:, :, None]
    return jnp.einsum('brc,brd->bcd', masked_rows, full_rows, precision=highest)

def scene_info(merged, sensitivity, width):
    basis = jnp.eye(width, dtype=jnp.float32)[None] + sensitivity.astype(jnp.float32)
    corner = merged[:, :width, :width]
    side = merged[:, :width, width:]
    tail = merged[:, width:, width:]
    mixed = jnp.einsum('sab,sbc->sac', corner, basis, precision=highest)
    corner_new = jnp.einsum('sba,sbc->sac', basis, mixed, precision=highest)
    side_new = jnp.einsum('sba,sbc->sac', basis, side, precision=highest)
    upper_half = jnp.concatenate([corner_new, side_new], 2)
    lower_half = jnp.concatenate([jnp.transpose(side_new, (0, 2, 1)), tail], 2)
    return jnp.concatenate([upper_half, lower_half], 1)

def factor_scenes(information, damping, width):
    identity = jnp.eye(width, dtype=jnp.float32)
    corner = information[:, :width, :width] + damping[:, None, None] * identity
    chol_lower = jnp.linalg.cholesky(corner)
    cross = jax.scipy.linalg.solve_triangular(chol_lower, information[:, :width, width:], lower=True)
    reduced = information[:, width:, width:] - jnp.einsum('sab,sac->sbc', cross, cross, precision=highest)
    out_rows = jnp.concatenate([jnp.transpose(chol_lower, (0, 2, 1)), cross], 2)
    return (out_rows, jnp.sum(reduced, 0))

def reference(tie_rows, point_counts, pattern, sensitivity, damping, prior):
    block_grams = block_gram(tie_rows, point_counts)
    grams_flat = block_grams.reshape(NBLK, COLS * COLS)

    def group(items):
        group_pattern, group_sens, group_damp = items
        merged = jnp.dot(group_pattern.astype(jnp.float32), grams_flat, precision=highest).reshape(SC_SHARD, COLS, COLS)
        information = scene_info(merged, group_sens, SPLINE)
        return factor_scenes(information, group_damp, SPLINE)
    rows_out, reduced_parts = lax.map(group, (pattern.reshape(N_SCENE, SC_SHARD, NBLK), sensitivity.reshape(N_SCENE, SC_SHARD, SPLINE, SPLINE), damping.reshape(N_SCENE, SC_SHARD)))
    scene_rows = rows_out.reshape(NSC, SPLINE, COLS)
    total = jnp.diag(prior) + jnp.sum(reduced_parts, 0) / NSC
    return (scene_rows, jnp.transpose(jnp.linalg.cholesky(total)))
```

```python
import functools

import jax
import jax.numpy as jnp
from jax import lax
from jax.experimental import pallas as pl
from jax.experimental.pallas import tpu as pltpu
from jax.sharding import PartitionSpec as P

SPLINE = 192
SHARED = 64
COLS = 256
PACK = 264
PANEL = 32
N_PANEL = SPLINE // PANEL
UNROLL = 4
DEPTH = 16
f32 = jnp.float32
bf16 = jnp.bfloat16


def iota(shape, axis):
    return lax.broadcasted_iota(jnp.int32, shape, axis)


def split(x):
    high = x.astype(bf16)
    return high, (x - high.astype(f32)).astype(bf16)


def dot(a, b, contract=((1,), (0,))):
    return lax.dot_general(a, b, (contract, ((), ())), preferred_element_type=f32)


def dot3(a, b, contract=((1,), (0,))):
    a_high, a_low = split(a)
    b_high, b_low = split(b)
    return dot(a_high, b_high, contract) + (dot(a_low, b_high, contract) + dot(a_high, b_low, contract))


def outer_panel(left_high, left_low, right_high, right_low):
    left = jnp.concatenate([left_high, left_low, left_high, left_low], 0)
    right = jnp.concatenate([right_high, right_high, right_low, right_low], 0)
    return dot(left, right, ((0,), (0,)))


def invert_lower(packed):
    lane = iota((PANEL, 128), 1)
    group = lane - lax.rem(lane, PANEL)
    blocks = PANEL // 8
    sub = iota((8, 128), 0)
    columns = []
    for j in range(PANEL):
        wide = jnp.take_along_axis(packed, group + j, axis=1)
        columns.append([wide[8 * v:8 * v + 8] for v in range(blocks)])
    ident = (iota((PANEL, 128), 0) == lax.rem(lane, PANEL)).astype(f32)
    x = [ident[8 * v:8 * v + 8] for v in range(blocks)]

    def spread(block, at):
        return jnp.broadcast_to(block[at:at + 1], (8, 128))

    for k in range(PANEL):
        kv, ks = divmod(k, 8)
        scale = lax.rsqrt(spread(columns[k][kv], ks))
        lower = [None] * blocks
        for v in range(kv, blocks):
            lower[v] = columns[k][v] * scale
        for j in range(k + 1, PANEL):
            jv, js = divmod(j, 8)
            factor = spread(lower[jv], js)
            for v in range(jv, blocks):
                columns[j][v] = columns[j][v] - lower[v] * factor
        row = spread(x[kv], ks) * scale
        for v in range(kv, blocks):
            if v == kv:
                below = jnp.where(sub > ks, lower[v], 0.0)
                x[v] = jnp.where(sub == ks, row, x[v] - below * row)
            else:
                x[v] = x[v] - lower[v] * row
    return jnp.concatenate(x, 0)


def factor_kernel(damp_ref, own_ref, below_refs, above_refs, sens_ref, rows_ref, sum_ref, work):
    owned = rows_ref.shape[0]
    r1, c1 = iota((128, 128), 0), iota((128, 128), 1)
    tail_sum = jnp.zeros((SHARED, 128), f32)
    for s in range(owned):
        arrived, at = (below_refs, s) if s < owned // 2 else (above_refs, s - owned // 2)
        part = own_ref[s] + (arrived[0][at] + arrived[1][at])
        packed, side = part[:128], part[128:256]
        diagonal = jnp.sum(part[256:264], axis=0, keepdims=True)
        turned = packed.T
        first = jnp.where(r1 <= c1, packed, turned)
        last = jnp.where(r1 > c1, packed, jnp.where(r1 == c1, diagonal, turned))
        tail_sum = tail_sum + last[SHARED:]
        top = jnp.concatenate([
            jnp.concatenate([first, side], 1),
            jnp.concatenate([side.T[:SPLINE - 128], last[:SPLINE - 128]], 1),
        ], 0)
        sens = sens_ref[s]
        wide_sens = jnp.concatenate([sens, jnp.zeros((SPLINE, SHARED), bf16)], 1)
        high, low = split(top[:, :SPLINE])
        mixed = top + dot(high, wide_sens) + dot(low, wide_sens)
        high, low = split(mixed)
        both = ((0,), (0,))
        square = jnp.concatenate([wide_sens, jnp.zeros((COLS - SPLINE, COLS), bf16)], 0)
        pad = jnp.zeros((COLS - SPLINE, COLS), bf16)
        high, low = jnp.concatenate([high, pad], 0), jnp.concatenate([low, pad], 0)
        info = mixed + (dot(square, high, both) + dot(square, low, both))[:SPLINE]
        info = info + jnp.where(iota((SPLINE, COLS), 0) == iota((SPLINE, COLS), 1), damp_ref[s], 0.0)
        for p in range(N_PANEL):
            work[p, s * PANEL:(s + 1) * PANEL] = info[p * PANEL:(p + 1) * PANEL]
    tail_sum = tail_sum[:, SHARED:]

    lane = iota((PANEL, 128), 1)
    same = (r1 // PANEL) == (c1 // PANEL)
    row_in = lax.rem(iota((128, COLS), 0), PANEL)
    col_in = iota((128, COLS), 1)
    for p in range(N_PANEL):
        half, inner = divmod(p * PANEL, 128)
        current = work[p]
        packed = jnp.zeros((PANEL, 128), f32)
        for s in range(owned):
            piece = current[s * PANEL:(s + 1) * PANEL, half * 128:(half + 1) * 128]
            shift = (s * PANEL - inner) % 128
            if shift:
                piece = pltpu.roll(piece, shift, 1)
            packed = jnp.where(lane // PANEL == s, piece, packed)
        inverse = invert_lower(packed)
        spread = jnp.where(same, jnp.concatenate([inverse] * (128 // PANEL), 0), 0.0)
        rows = dot3(spread, current)
        rows = jnp.where(col_in >= row_in + p * PANEL, rows, 0.0)
        for s in range(owned):
            rows_ref[s, p * PANEL:(p + 1) * PANEL] = rows[s * PANEL:(s + 1) * PANEL]
        high, low = split(rows)
        start = ((p + 1) * PANEL) // 128 * 128
        if p + 1 < N_PANEL:
            for s in range(owned):
                at = slice(s * PANEL, (s + 1) * PANEL)
                update = outer_panel(high[at, start:], low[at, start:], high[at], low[at])
                for q in range(p + 1, N_PANEL):
                    work[q, at] = work[q, at] - update[q * PANEL - start:(q + 1) * PANEL - start]
        cross_high, cross_low = high[:, 128:], low[:, 128:]
        both = ((0,), (0,))
        outer = dot(cross_high, cross_high, both) + (dot(cross_high, cross_low, both) + dot(cross_low, cross_high, both))
        tail_sum = tail_sum - outer[SHARED:, SHARED:]
    sum_ref[...] = tail_sum


def factor_scenes(own, below, above, sens, damping):
    owned = damping.shape[0]
    vmem = pl.BlockSpec(memory_space=pltpu.VMEM)

    def kernel(damp_ref, own_ref, b0, b1, a0, a1, *rest):
        factor_kernel(damp_ref, own_ref, (b0, b1), (a0, a1), *rest)

    return pl.pallas_call(
        kernel,
        out_shape=(
            jax.ShapeDtypeStruct((owned, SPLINE, COLS), f32),
            jax.ShapeDtypeStruct((SHARED, SHARED), f32),
        ),
        in_specs=[pl.BlockSpec(memory_space=pltpu.SMEM)] + [vmem] * 6,
        out_specs=(vmem, vmem),
        scratch_shapes=[pltpu.VMEM((N_PANEL, owned * PANEL, COLS), f32)],
        compiler_params=pltpu.CompilerParams(vmem_limit_bytes=32 * 1024 * 1024),
        name="factor_scenes",
    )(damping, own, *below, *above, sens)


def total_kernel(n_parts, count, *refs):
    prior_ref = refs[0]
    out_ref = refs[-1]
    total = refs[1][...]
    for other in refs[2:-1]:
        total = total + other[...]
    total = total / count
    r, c = iota((SHARED, SHARED), 0), iota((SHARED, SHARED), 1)
    total = total + jnp.where(r == c, prior_ref[...], 0.0)
    pad = jnp.zeros((SHARED, 128 - SHARED), f32)
    wide = jnp.concatenate([total, pad], 1)
    top, bottom = wide[:PANEL], wide[PANEL:]
    lane = iota((PANEL, 128), 1)
    row = iota((PANEL, 128), 0)
    inverse = invert_lower(top)
    upper = dot3(jnp.where(lane < PANEL, inverse, 0.0)[:, :PANEL], top)
    upper = jnp.where(lane >= row, upper, 0.0)
    high, low = split(upper)
    bottom = bottom - outer_panel(high, low, high, low)[PANEL:SHARED]
    moved = pltpu.roll(bottom, 128 - PANEL, 1)
    inverse = invert_lower(moved)
    lower = dot3(inverse[:, :PANEL], bottom)
    lower = jnp.where(lane >= row + PANEL, lower, 0.0)
    out_ref[...] = jnp.concatenate([upper[:, :SHARED], lower[:, :SHARED]], 0)


def factor_total(parts, prior, count):
    vmem = pl.BlockSpec(memory_space=pltpu.VMEM)
    return pl.pallas_call(
        functools.partial(total_kernel, len(parts), count),
        out_shape=jax.ShapeDtypeStruct((SHARED, SHARED), f32),
        in_specs=[vmem] * (1 + len(parts)),
        out_specs=vmem,
        name="factor_total",
    )(prior.reshape(1, SHARED), *parts)


def gram_kernel(groups, me_ref, pat_ref, cnt_ref, tie_ref, *rest):
    n_out = len(groups)
    outs = rest[:n_out]
    acc, held, pairs, sems = rest[n_out:]
    n_block = tie_ref.shape[0]
    slots = [(distance, scene) for distance, scenes in groups for scene in scenes]
    n_slot = len(slots)
    ways = 4
    found = jnp.int32(0)
    for slot, (distance, scene) in enumerate(slots):
        row = lax.rem(me_ref[0] + distance, ways) * (pat_ref.shape[0] // ways) + scene

        def some(i, found, slot=slot, row=row):
            for j in range(8):
                block = i * 8 + j
                pairs[found] = slot * 1024 + block
                found = found + pat_ref[row, block]
            return found

        found = lax.fori_loop(0, n_block // 8, some, found)
    for j in range(UNROLL):
        pairs[found + j] = n_slot * 1024
    rounds = lax.div(found + (UNROLL - 1), UNROLL)
    rings = DEPTH // UNROLL

    def fetch(index, slot):
        return pltpu.make_async_copy(
            tie_ref.at[lax.bitwise_and(pairs[index], 1023)], held.at[slot], sems.at[slot]
        )

    for g in range(rings):
        @pl.when(g < rounds)
        def _():
            for j in range(UNROLL):
                fetch(g * UNROLL + j, g * UNROLL + j).start()

    acc[...] = jnp.zeros_like(acc)
    row_at = iota((COLS, COLS), 0)
    r1, c1 = iota((128, 128), 0), iota((128, 128), 1)
    both = ((0,), (0,))

    def step(i, carry):
        base = lax.rem(i, rings) * UNROLL
        for j in range(UNROLL):
            fetch(i * UNROLL + j, base + j).wait()
        for j in range(UNROLL):
            pair = pairs[i * UNROLL + j]
            slot = lax.shift_right_logical(pair, 10)
            rows = held[base + j]
            kept = jnp.where(row_at < 2 * cnt_ref[lax.bitwise_and(pair, 1023)], rows, jnp.zeros_like(rows))
            top = dot(kept[:, :128], rows, both)
            last = dot(kept[:, 128:], rows[:, 128:], both)
            acc[slot, 0:128] += jnp.where(r1 <= c1, top[:, :128], last)
            acc[slot, 128:256] += top[:, 128:]
            acc[slot, 256:264] += jnp.sum(jnp.where(r1 == c1, last, 0.0).reshape(16, 8, 128), axis=0)

        @pl.when(i + rings < rounds)
        def _():
            for j in range(UNROLL):
                fetch((i + rings) * UNROLL + j, base + j).start()
        return carry

    lax.fori_loop(0, rounds, step, 0)
    at = 0
    for out, (distance, scenes) in zip(outs, groups):
        out[...] = acc[at:at + len(scenes)]
        at += len(scenes)


def partial_grams(me, pattern, counts, tie_rows, groups):
    smem = pl.BlockSpec(memory_space=pltpu.SMEM)
    vmem = pl.BlockSpec(memory_space=pltpu.VMEM)
    n_slot = sum(len(scenes) for _, scenes in groups)
    n_pairs = n_slot * tie_rows.shape[0] + UNROLL
    return pl.pallas_call(
        functools.partial(gram_kernel, groups),
        out_shape=[jax.ShapeDtypeStruct((len(scenes), PACK, 128), f32) for _, scenes in groups],
        in_specs=[smem, smem, smem, pl.BlockSpec(memory_space=pl.ANY)],
        out_specs=[vmem] * len(groups),
        scratch_shapes=[
            pltpu.VMEM((n_slot + 1, PACK, 128), f32),
            pltpu.VMEM((DEPTH, COLS, COLS), bf16),
            pltpu.SMEM(((n_pairs + 127) // 128 * 128,), jnp.int32),
            pltpu.SemaphoreType.DMA((DEPTH,)),
        ],
        compiler_params=pltpu.CompilerParams(vmem_limit_bytes=56 * 1024 * 1024),
        name="partial_grams",
    )(me, pattern, counts, tie_rows)


def ring(step, size):
    return [(i, (i + step) % size) for i in range(size)]


def swap(bits, size):
    return [(i, i ^ bits) for i in range(size)]


def on_device(tie_rows, point_counts, pattern, sensitivity, damping, prior):
    owned = damping.shape[0]
    ways = lax.axis_size("tie")
    me = lax.axis_index("tie")
    me_word = me.reshape(1).astype(jnp.int32)
    near, far = (0, 1), (2, 3)
    up = functools.partial(lax.ppermute, axis_name="tie", perm=ring(1, ways))
    down = functools.partial(lax.ppermute, axis_name="tie", perm=ring(-1, ways))

    far_up, far_down = partial_grams(me_word, pattern, point_counts, tie_rows, ((2, near), (2, far)))
    came_up, came_down = up(far_up), down(far_down)
    up_now, up_later, down_now, down_later, own = partial_grams(
        me_word, pattern, point_counts, tie_rows,
        ((1, far), (1, near), (3, near), (3, far), (0, near + far)),
    )
    sens = lax.dynamic_slice_in_dim(sensitivity, me * owned, owned, 0)
    got_up, got_down = up(up_now), down(down_now)
    last_up, last_down = up(up_later + came_up), down(down_later + came_down)
    scene_rows, reduced = factor_scenes(own, (last_up, got_down), (got_up, last_down), sens, damping)

    n_scene = lax.axis_size("scene")
    total = reduced
    for axis, bits in (("scene", 1), ("tie", 1), ("tie", 3), ("scene", 2), ("scene", 6), ("scene", 8)):
        total = total + lax.ppermute(total, axis, swap(bits, lax.axis_size(axis)))
    other = lax.ppermute(total, "scene", swap(24, n_scene))
    global_factor = factor_total((total, other), prior, float(owned * n_scene * ways))
    return (scene_rows, global_factor)


def solution(mesh):
    placed = (
        P("tie", None, None),
        P("tie"),
        P("scene", "tie"),
        P("scene", None, None),
        P(("scene", "tie")),
        P(),
    )
    return jax.shard_map(
        on_device,
        mesh=mesh,
        in_specs=placed,
        out_specs=(P(("scene", "tie"), None, None), P()),
        check_vma=False,
    )
```

```python
import functools

import jax
import jax.numpy as jnp
from jax import lax
from jax.experimental import pallas as pl
from jax.experimental.pallas import tpu as pltpu
from jax.sharding import PartitionSpec as P

SPLINE = 192
SHARED = 64
COLS = 256
PACK = 264
PANEL = 32
N_PANEL = SPLINE // PANEL
UNROLL = 8
DEPTH = 32
WORD = 24
f32 = jnp.float32
bf16 = jnp.bfloat16


def iota(shape, axis):
    return lax.broadcasted_iota(jnp.int32, shape, axis)


def split(x):
    high = x.astype(bf16)
    return high, (x - high.astype(f32)).astype(bf16)


def dot(a, b, contract=((1,), (0,))):
    return lax.dot_general(a, b, (contract, ((), ())), preferred_element_type=f32)


def dot3(a, b, contract=((1,), (0,))):
    a_high, a_low = split(a)
    b_high, b_low = split(b)
    return dot(a_high, b_high, contract) + (dot(a_low, b_high, contract) + dot(a_high, b_low, contract))


def outer_panel(left_high, left_low, right_high, right_low):
    left = jnp.concatenate([left_high, left_low, left_high, left_low], 0)
    right = jnp.concatenate([right_high, right_high, right_low, right_low], 0)
    return dot(left, right, ((0,), (0,)))


def invert_lower(packed):
    lane = iota((PANEL, 128), 1)
    group = lane - lax.rem(lane, PANEL)
    blocks = PANEL // 8
    sub = iota((8, 128), 0)
    columns = []
    for j in range(PANEL):
        wide = jnp.take_along_axis(packed, group + j, axis=1)
        columns.append([wide[8 * v:8 * v + 8] for v in range(blocks)])
    ident = (iota((PANEL, 128), 0) == lax.rem(lane, PANEL)).astype(f32)
    x = [ident[8 * v:8 * v + 8] for v in range(blocks)]

    def spread(block, at):
        return jnp.broadcast_to(block[at:at + 1], (8, 128))

    for k in range(PANEL):
        kv, ks = divmod(k, 8)
        scale = lax.rsqrt(spread(columns[k][kv], ks))
        lower = [None] * blocks
        for v in range(kv, blocks):
            lower[v] = columns[k][v] * scale
        for j in range(k + 1, PANEL):
            jv, js = divmod(j, 8)
            factor = spread(lower[jv], js)
            for v in range(jv, blocks):
                columns[j][v] = columns[j][v] - lower[v] * factor
        row = spread(x[kv], ks) * scale
        for v in range(kv, blocks):
            if v == kv:
                below = jnp.where(sub > ks, lower[v], 0.0)
                x[v] = jnp.where(sub == ks, row, x[v] - below * row)
            else:
                x[v] = x[v] - lower[v] * row
    return jnp.concatenate(x, 0)


def factor_kernel(damp_ref, own_ref, below_refs, above_refs, sens_ref, rows_ref, sum_ref, work):
    owned = rows_ref.shape[0]
    r1, c1 = iota((128, 128), 0), iota((128, 128), 1)
    tail_sum = jnp.zeros((SHARED, 128), f32)
    for s in range(owned):
        arrived, at = (below_refs, s) if s < owned // 2 else (above_refs, s - owned // 2)
        part = own_ref[s] + (arrived[0][at] + arrived[1][at])
        packed, side = part[:128], part[128:256]
        diagonal = jnp.sum(part[256:264], axis=0, keepdims=True)
        turned = packed.T
        first = jnp.where(r1 <= c1, packed, turned)
        last = jnp.where(r1 > c1, packed, jnp.where(r1 == c1, diagonal, turned))
        tail_sum = tail_sum + last[SHARED:]
        top = jnp.concatenate([
            jnp.concatenate([first, side], 1),
            jnp.concatenate([side.T[:SPLINE - 128], last[:SPLINE - 128]], 1),
        ], 0)
        sens = sens_ref[s]
        wide_sens = jnp.concatenate([sens, jnp.zeros((SPLINE, SHARED), bf16)], 1)
        high, low = split(top[:, :SPLINE])
        mixed = top + dot(high, wide_sens) + dot(low, wide_sens)
        high, low = split(mixed)
        both = ((0,), (0,))
        square = jnp.concatenate([wide_sens, jnp.zeros((COLS - SPLINE, COLS), bf16)], 0)
        pad = jnp.zeros((COLS - SPLINE, COLS), bf16)
        high, low = jnp.concatenate([high, pad], 0), jnp.concatenate([low, pad], 0)
        info = mixed + (dot(square, high, both) + dot(square, low, both))[:SPLINE]
        info = info + jnp.where(iota((SPLINE, COLS), 0) == iota((SPLINE, COLS), 1), damp_ref[s], 0.0)
        for p in range(N_PANEL):
            work[p, s * PANEL:(s + 1) * PANEL] = info[p * PANEL:(p + 1) * PANEL]

    lane = iota((PANEL, 128), 1)
    same = (r1 // PANEL) == (c1 // PANEL)
    row_in = lax.rem(iota((128, COLS), 0), PANEL)
    col_in = iota((128, COLS), 1)
    for p in range(N_PANEL):
        half, inner = divmod(p * PANEL, 128)
        current = work[p]
        packed = jnp.zeros((PANEL, 128), f32)
        for s in range(owned):
            piece = current[s * PANEL:(s + 1) * PANEL, half * 128:(half + 1) * 128]
            shift = (s * PANEL - inner) % 128
            if shift:
                piece = pltpu.roll(piece, shift, 1)
            packed = jnp.where(lane // PANEL == s, piece, packed)
        inverse = invert_lower(packed)
        spread = jnp.where(same, jnp.concatenate([inverse] * (128 // PANEL), 0), 0.0)
        rows = dot3(spread, current)
        rows = jnp.where(col_in >= row_in + p * PANEL, rows, 0.0)
        for s in range(owned):
            rows_ref[s, p * PANEL:(p + 1) * PANEL] = rows[s * PANEL:(s + 1) * PANEL]
        high, low = split(rows)
        start = ((p + 1) * PANEL) // 128 * 128
        if p + 1 < N_PANEL:
            for s in range(owned):
                at = slice(s * PANEL, (s + 1) * PANEL)
                update = outer_panel(high[at, start:], low[at, start:], high[at], low[at])
                for q in range(p + 1, N_PANEL):
                    work[q, at] = work[q, at] - update[q * PANEL - start:(q + 1) * PANEL - start]
        cross_high, cross_low = high[:, 128:], low[:, 128:]
        both = ((0,), (0,))
        outer = dot(cross_high, cross_high, both) + (dot(cross_high, cross_low, both) + dot(cross_low, cross_high, both))
        tail_sum = tail_sum - outer[SHARED:]
    sum_ref[...] = jnp.where(lane < SHARED, pltpu.roll(tail_sum[:PANEL], SHARED, 1), tail_sum[PANEL:])


def factor_scenes(own, below, above, sens, damping):
    owned = damping.shape[0]
    vmem = pl.BlockSpec(memory_space=pltpu.VMEM)

    def kernel(damp_ref, own_ref, b0, b1, a0, a1, *rest):
        factor_kernel(damp_ref, own_ref, (b0, b1), (a0, a1), *rest)

    return pl.pallas_call(
        kernel,
        out_shape=(
            jax.ShapeDtypeStruct((owned, SPLINE, COLS), f32),
            jax.ShapeDtypeStruct((PANEL, 128), f32),
        ),
        in_specs=[pl.BlockSpec(memory_space=pltpu.SMEM)] + [vmem] * 6,
        out_specs=(vmem, vmem),
        scratch_shapes=[pltpu.VMEM((N_PANEL, owned * PANEL, COLS), f32)],
        compiler_params=pltpu.CompilerParams(vmem_limit_bytes=32 * 1024 * 1024),
        name="factor_scenes",
    )(damping, own, *below, *above, sens)


def total_kernel(count, prior_ref, parts_ref, out_ref):
    total = parts_ref[0]
    for i in range(1, parts_ref.shape[0]):
        total = total + parts_ref[i]
    total = total / count
    lane, row = iota((PANEL, 128), 1), iota((PANEL, 128), 0)
    prior = jnp.concatenate([prior_ref[...], prior_ref[...]], 1)
    total = total + jnp.where((lane == row) | (lane == row + SHARED + PANEL), prior, 0.0)
    first = jnp.where(lane < PANEL, invert_lower(total), 0.0)
    upper = dot3(first[:, :PANEL], total)
    upper = jnp.where((lane >= row) & (lane < SHARED), upper, 0.0)
    bottom = pltpu.roll(total, SHARED, 1)
    high, low = split(upper)
    bottom = jnp.where(lane < SHARED, bottom - outer_panel(high, low, high, low)[PANEL:SHARED], 0.0)
    second = jnp.where(lane < PANEL, invert_lower(pltpu.roll(bottom, 128 - PANEL, 1)), 0.0)
    lower = dot3(second[:, :PANEL], bottom)
    lower = jnp.where(lane >= row + PANEL, lower, 0.0)
    out_ref[...] = jnp.concatenate([upper[:, :SHARED], lower[:, :SHARED]], 0)


def factor_total(parts, prior, count):
    vmem = pl.BlockSpec(memory_space=pltpu.VMEM)
    return pl.pallas_call(
        functools.partial(total_kernel, count),
        out_shape=jax.ShapeDtypeStruct((SHARED, SHARED), f32),
        in_specs=[vmem] * 2,
        out_specs=vmem,
        name="factor_total",
    )(prior.reshape(1, SHARED), parts)


def gram_kernel(groups, n_begin, me_ref, bits_ref, cnt_ref, tie_ref, *rest):
    n_out = len(groups)
    begin_refs, rest = rest[:n_begin], rest[n_begin:]
    outs = rest[:n_out]
    acc, held, pairs, sems = rest[n_out:]
    slots = [(distance, scene) for distance, scenes in groups for scene in scenes]
    n_slot = len(slots)
    ways = 4
    rings = DEPTH // UNROLL

    def fetch(block, slot):
        return pltpu.make_async_copy(tie_ref.at[block], held.at[slot], sems.at[slot])

    def note(found, pair):
        pairs[found] = pair

        @pl.when(found < DEPTH)
        def _():
            fetch(lax.bitwise_and(pair, 1023), found).start()

    found = jnp.int32(0)
    for slot, (distance, scene) in enumerate(slots):
        row = lax.rem(me_ref[0] + distance, ways) * (bits_ref.shape[1] // ways) + scene
        for w in range(bits_ref.shape[0]):

            def some(carry, slot=slot, w=w):
                word, found = carry
                low = lax.bitwise_and(word, -word)
                note(found, slot * 1024 + w * WORD + 31 - lax.clz(low))
                return word - low, found + 1

            _, found = lax.while_loop(lambda carry: carry[0] != 0, some, (bits_ref[w, row], found))
    rounds = lax.div(found + (UNROLL - 1), UNROLL)
    for j in range(UNROLL - 1):
        @pl.when(found + j < rounds * UNROLL)
        def _(j=j):
            note(found + j, n_slot * 1024)

    if n_begin:
        at = 0
        for begin_ref in begin_refs:
            acc[at:at + begin_ref.shape[0]] = begin_ref[...]
            at += begin_ref.shape[0]
        acc[at] = jnp.zeros_like(acc[at])
    else:
        acc[...] = jnp.zeros_like(acc)
    row_at = iota((COLS, COLS), 0)
    r1, c1 = iota((128, 128), 0), iota((128, 128), 1)
    both = ((0,), (0,))

    def step(i, carry):
        base = lax.rem(i, rings) * UNROLL
        for j in range(UNROLL):
            fetch(0, base + j).wait()
        for j in range(UNROLL):
            pair = pairs[i * UNROLL + j]
            slot = lax.shift_right_logical(pair, 10)
            rows = held[base + j]
            kept = jnp.where(row_at < 2 * cnt_ref[lax.bitwise_and(pair, 1023)], rows, jnp.zeros_like(rows))
            top = dot(kept[:, :128], rows, both)
            last = dot(kept[:, 128:], rows[:, 128:], both)
            acc[slot, 0:128] += jnp.where(r1 <= c1, top[:, :128], last)
            acc[slot, 128:256] += top[:, 128:]
            acc[slot, 256:264] += jnp.sum(jnp.where(r1 == c1, last, 0.0).reshape(16, 8, 128), axis=0)

        @pl.when(i + rings < rounds)
        def _():
            for j in range(UNROLL):
                fetch(lax.bitwise_and(pairs[(i + rings) * UNROLL + j], 1023), base + j).start()
        return carry

    lax.fori_loop(0, rounds, step, 0)
    at = 0
    for out, (distance, scenes) in zip(outs, groups):
        out[...] = acc[at:at + len(scenes)]
        at += len(scenes)


def partial_grams(me, bits, counts, tie_rows, groups, begin=()):
    smem = pl.BlockSpec(memory_space=pltpu.SMEM)
    vmem = pl.BlockSpec(memory_space=pltpu.VMEM)
    n_slot = sum(len(scenes) for _, scenes in groups)
    n_pairs = n_slot * tie_rows.shape[0] + UNROLL
    return pl.pallas_call(
        functools.partial(gram_kernel, groups, len(begin)),
        out_shape=[jax.ShapeDtypeStruct((len(scenes), PACK, 128), f32) for _, scenes in groups],
        in_specs=[smem, smem, smem, pl.BlockSpec(memory_space=pl.ANY)] + [vmem] * len(begin),
        out_specs=[vmem] * len(groups),
        scratch_shapes=[
            pltpu.VMEM((n_slot + 1, PACK, 128), f32),
            pltpu.VMEM((DEPTH, COLS, COLS), bf16),
            pltpu.SMEM(((n_pairs + 127) // 128 * 128,), jnp.int32),
            pltpu.SemaphoreType.DMA((DEPTH,)),
        ],
        compiler_params=pltpu.CompilerParams(vmem_limit_bytes=52 * 1024 * 1024),
        name="partial_grams",
    )(me, bits, counts, tie_rows, *begin)


def pattern_bits(pattern):
    n_scene, n_block = pattern.shape
    words = -(-n_block // WORD)
    block = jnp.arange(n_block, dtype=jnp.int32)
    bit = jnp.left_shift(1, block % WORD)
    weight = jnp.where(block[None, :] // WORD == jnp.arange(words, dtype=jnp.int32)[:, None], bit[None, :], 0)
    return jnp.sum(pattern[None, :, :] * weight[:, None, :], axis=2)


def ring(step, size):
    return [(i, (i + step) % size) for i in range(size)]


def share(value, axes, groups):
    sent = jnp.broadcast_to(value[None], (len(groups[0]),) + value.shape)
    return lax.all_to_all(sent, axes, 0, 0, axis_index_groups=groups, tiled=True)


def on_device(tie_rows, point_counts, pattern, sensitivity, damping, prior):
    owned = damping.shape[0]
    ways = lax.axis_size("tie")
    me = lax.axis_index("tie")
    me_word = me.reshape(1).astype(jnp.int32)
    near, far = (0, 1), (2, 3)
    up = functools.partial(lax.ppermute, axis_name="tie", perm=ring(1, ways))
    down = functools.partial(lax.ppermute, axis_name="tie", perm=ring(-1, ways))

    bits = pattern_bits(pattern)
    far_up, far_down = partial_grams(me_word, bits, point_counts, tie_rows, ((2, near), (2, far)))
    came_up, came_down = up(far_up), down(far_down)
    up_now, down_now = partial_grams(me_word, bits, point_counts, tie_rows, ((1, far), (3, near)))
    sens = lax.dynamic_slice_in_dim(sensitivity, me * owned, owned, 0)
    got_up, got_down = up(up_now), down(down_now)
    up_later, down_later = partial_grams(
        me_word, bits, point_counts, tie_rows, ((1, near), (3, far)), (came_up, came_down)
    )
    last_up, last_down = up(up_later), down(down_later)
    (own,) = partial_grams(me_word, bits, point_counts, tie_rows, ((0, near + far),))
    scene_rows, reduced = factor_scenes(own, (last_up, got_down), (got_up, last_down), sens, damping)

    n_scene = lax.axis_size("scene")
    plane = [[i for i in range(n_scene) if i % 2 == core] for core in range(2)]
    line = [list(range(ways))]
    chip = reduced + lax.ppermute(reduced, "scene", [(i, i ^ 1) for i in range(n_scene)])
    shares = share(chip, "scene", plane)
    total_parts = share(jnp.sum(shares, 0), "tie", line)
    global_factor = factor_total(total_parts, prior, float(owned * n_scene * ways))
    return (scene_rows, global_factor)


def solution(mesh):
    placed = (
        P("tie", None, None),
        P("tie"),
        P("scene", "tie"),
        P("scene", None, None),
        P(("scene", "tie")),
        P(),
    )
    return jax.shard_map(
        on_device,
        mesh=mesh,
        in_specs=placed,
        out_specs=(P(("scene", "tie"), None, None), P()),
        check_vma=False,
    )
```

```python
import functools

import jax
import jax.numpy as jnp
from jax import lax
from jax.experimental import pallas as pl
from jax.experimental.pallas import tpu as pltpu
from jax.sharding import PartitionSpec as P

SPLINE = 192
SHARED = 64
COLS = 256
PACK = 264
PANEL = 32
N_PANEL = SPLINE // PANEL
UNROLL = 8
DEPTH = 32
WORD = 24
f32 = jnp.float32
bf16 = jnp.bfloat16


def iota(shape, axis):
    return lax.broadcasted_iota(jnp.int32, shape, axis)


def split(x):
    high = x.astype(bf16)
    return high, (x - high.astype(f32)).astype(bf16)


def dot(a, b, contract=((1,), (0,))):
    return lax.dot_general(a, b, (contract, ((), ())), preferred_element_type=f32)


def dot3(a, b, contract=((1,), (0,))):
    a_high, a_low = split(a)
    b_high, b_low = split(b)
    return dot(a_high, b_high, contract) + (dot(a_low, b_high, contract) + dot(a_high, b_low, contract))


def outer_panel(left_high, left_low, right_high, right_low):
    left = jnp.concatenate([left_high, left_low, left_high, left_low], 0)
    right = jnp.concatenate([right_high, right_high, right_low, right_low], 0)
    return dot(left, right, ((0,), (0,)))


def invert_lower(packed):
    lane = iota((PANEL, 128), 1)
    group = lane - lax.rem(lane, PANEL)
    blocks = PANEL // 8
    sub = iota((8, 128), 0)
    columns = []
    for j in range(PANEL):
        wide = jnp.take_along_axis(packed, group + j, axis=1)
        columns.append([wide[8 * v:8 * v + 8] for v in range(blocks)])
    ident = (iota((PANEL, 128), 0) == lax.rem(lane, PANEL)).astype(f32)
    x = [ident[8 * v:8 * v + 8] for v in range(blocks)]

    def spread(block, at):
        return jnp.broadcast_to(block[at:at + 1], (8, 128))

    scales = [jnp.ones((8, 128), f32) for _ in range(blocks)]
    for k in range(PANEL):
        kv, ks = divmod(k, 8)
        pivot = spread(columns[k][kv], ks)
        inverse = 1.0 / pivot
        scales[kv] = jnp.where(sub == ks, lax.rsqrt(pivot), scales[kv])
        lower = [None] * kv + [columns[k][v] * inverse for v in range(kv, blocks)]
        for j in range(k + 1, PANEL):
            jv, js = divmod(j, 8)
            factor = spread(columns[k][jv], js)
            for v in range(jv, blocks):
                if j == k + 1:
                    columns[j][v] = columns[j][v] - (columns[k][v] * factor) * inverse
                else:
                    columns[j][v] = columns[j][v] - lower[v] * factor
        row = spread(x[kv], ks)
        for v in range(kv, blocks):
            below = jnp.where(sub > ks, lower[v], 0.0) if v == kv else lower[v]
            x[v] = x[v] - below * row
    x = [value * scale for value, scale in zip(x, scales)]
    return jnp.concatenate(x, 0)


def factor_kernel(damp_ref, own_ref, below_refs, above_refs, sens_ref, rows_ref, sum_ref, work):
    owned = rows_ref.shape[0]
    r1, c1 = iota((128, 128), 0), iota((128, 128), 1)
    tail_sum = jnp.zeros((SHARED, 128), f32)
    for s in range(owned):
        arrived, at = (below_refs, s) if s < owned // 2 else (above_refs, s - owned // 2)
        part = own_ref[s] + (arrived[0][at] + arrived[1][at])
        packed, side = part[:128], part[128:256]
        diagonal = jnp.sum(part[256:264], axis=0, keepdims=True)
        turned = packed.T
        first = jnp.where(r1 <= c1, packed, turned)
        last = jnp.where(r1 > c1, packed, jnp.where(r1 == c1, diagonal, turned))
        tail_sum = tail_sum + last[SHARED:]
        top = jnp.concatenate([
            jnp.concatenate([first, side], 1),
            jnp.concatenate([side.T[:SPLINE - 128], last[:SPLINE - 128]], 1),
        ], 0)
        sens = sens_ref[s]
        wide_sens = jnp.concatenate([sens, jnp.zeros((SPLINE, SHARED), bf16)], 1)
        high, low = split(top[:, :SPLINE])
        mixed = top + dot(high, wide_sens) + dot(low, wide_sens)
        high, low = split(mixed)
        both = ((0,), (0,))
        square = jnp.concatenate([wide_sens, jnp.zeros((COLS - SPLINE, COLS), bf16)], 0)
        pad = jnp.zeros((COLS - SPLINE, COLS), bf16)
        high, low = jnp.concatenate([high, pad], 0), jnp.concatenate([low, pad], 0)
        info = mixed + (dot(square, high, both) + dot(square, low, both))[:SPLINE]
        info = info + jnp.where(iota((SPLINE, COLS), 0) == iota((SPLINE, COLS), 1), damp_ref[s], 0.0)
        for p in range(N_PANEL):
            work[p, s * PANEL:(s + 1) * PANEL] = info[p * PANEL:(p + 1) * PANEL]

    lane = iota((PANEL, 128), 1)
    same = (r1 // PANEL) == (c1 // PANEL)
    row_in = lax.rem(iota((128, COLS), 0), PANEL)
    col_in = iota((128, COLS), 1)
    for p in range(N_PANEL):
        half, inner = divmod(p * PANEL, 128)
        current = work[p]
        packed = jnp.zeros((PANEL, 128), f32)
        for s in range(owned):
            piece = current[s * PANEL:(s + 1) * PANEL, half * 128:(half + 1) * 128]
            shift = (s * PANEL - inner) % 128
            if shift:
                piece = pltpu.roll(piece, shift, 1)
            packed = jnp.where(lane // PANEL == s, piece, packed)
        inverse = invert_lower(packed)
        spread = jnp.where(same, jnp.concatenate([inverse] * (128 // PANEL), 0), 0.0)
        rows = dot3(spread, current)
        rows = jnp.where(col_in >= row_in + p * PANEL, rows, 0.0)
        for s in range(owned):
            rows_ref[s, p * PANEL:(p + 1) * PANEL] = rows[s * PANEL:(s + 1) * PANEL]
        high, low = split(rows)
        start = ((p + 1) * PANEL) // 128 * 128
        if p + 1 < N_PANEL:
            for s in range(owned):
                at = slice(s * PANEL, (s + 1) * PANEL)
                update = outer_panel(high[at, start:], low[at, start:], high[at], low[at])
                for q in range(p + 1, N_PANEL):
                    work[q, at] = work[q, at] - update[q * PANEL - start:(q + 1) * PANEL - start]
        cross_high, cross_low = high[:, 128:], low[:, 128:]
        both = ((0,), (0,))
        outer = dot(cross_high, cross_high, both) + (dot(cross_high, cross_low, both) + dot(cross_low, cross_high, both))
        tail_sum = tail_sum - outer[SHARED:]
    sum_ref[...] = jnp.where(lane < SHARED, pltpu.roll(tail_sum[:PANEL], SHARED, 1), tail_sum[PANEL:])


def factor_scenes(own, below, above, sens, damping):
    owned = damping.shape[0]
    vmem = pl.BlockSpec(memory_space=pltpu.VMEM)

    def kernel(damp_ref, own_ref, b0, b1, a0, a1, *rest):
        factor_kernel(damp_ref, own_ref, (b0, b1), (a0, a1), *rest)

    return pl.pallas_call(
        kernel,
        out_shape=(
            jax.ShapeDtypeStruct((owned, SPLINE, COLS), f32),
            jax.ShapeDtypeStruct((PANEL, 128), f32),
        ),
        in_specs=[pl.BlockSpec(memory_space=pltpu.SMEM)] + [vmem] * 6,
        out_specs=(vmem, vmem),
        scratch_shapes=[pltpu.VMEM((N_PANEL, owned * PANEL, COLS), f32)],
        compiler_params=pltpu.CompilerParams(vmem_limit_bytes=32 * 1024 * 1024),
        name="factor_scenes",
    )(damping, own, *below, *above, sens)


def total_kernel(count, prior_ref, parts_ref, out_ref):
    total = parts_ref[0]
    for i in range(1, parts_ref.shape[0]):
        total = total + parts_ref[i]
    total = total / count
    lane, row = iota((PANEL, 128), 1), iota((PANEL, 128), 0)
    prior = jnp.concatenate([prior_ref[...], prior_ref[...]], 1)
    total = total + jnp.where((lane == row) | (lane == row + SHARED + PANEL), prior, 0.0)
    first = jnp.where(lane < PANEL, invert_lower(total), 0.0)
    upper = dot3(first[:, :PANEL], total)
    upper = jnp.where((lane >= row) & (lane < SHARED), upper, 0.0)
    bottom = pltpu.roll(total, SHARED, 1)
    high, low = split(upper)
    bottom = jnp.where(lane < SHARED, bottom - outer_panel(high, low, high, low)[PANEL:SHARED], 0.0)
    second = jnp.where(lane < PANEL, invert_lower(pltpu.roll(bottom, 128 - PANEL, 1)), 0.0)
    lower = dot3(second[:, :PANEL], bottom)
    lower = jnp.where(lane >= row + PANEL, lower, 0.0)
    out_ref[...] = jnp.concatenate([upper[:, :SHARED], lower[:, :SHARED]], 0)


def factor_total(parts, prior, count):
    vmem = pl.BlockSpec(memory_space=pltpu.VMEM)
    return pl.pallas_call(
        functools.partial(total_kernel, count),
        out_shape=jax.ShapeDtypeStruct((SHARED, SHARED), f32),
        in_specs=[vmem] * 2,
        out_specs=vmem,
        compiler_params=pltpu.CompilerParams(vmem_limit_bytes=8 * 1024 * 1024),
        name="factor_total",
    )(prior.reshape(1, SHARED), parts)


def gram_kernel(groups, n_begin, me_ref, bits_ref, cnt_ref, tie_ref, *rest):
    n_out = len(groups)
    begin_refs, rest = rest[:n_begin], rest[n_begin:]
    outs = rest[:n_out]
    acc, held, pairs, sems = rest[n_out:]
    slots = [(distance, scene) for distance, scenes in groups for scene in scenes]
    n_slot = len(slots)
    ways = 4
    rings = DEPTH // UNROLL

    def fetch(block, slot):
        return pltpu.make_async_copy(tie_ref.at[block], held.at[slot], sems.at[slot])

    def note(found, pair):
        pairs[found] = pair

        @pl.when(found < DEPTH)
        def _():
            fetch(lax.bitwise_and(pair, 1023), found).start()

    found = jnp.int32(0)
    for slot, (distance, scene) in enumerate(slots):
        row = lax.rem(me_ref[0] + distance, ways) * (bits_ref.shape[1] // ways) + scene
        for w in range(bits_ref.shape[0]):

            def some(carry, slot=slot, w=w):
                word, found = carry
                low = lax.bitwise_and(word, -word)
                note(found, slot * 1024 + w * WORD + 31 - lax.clz(low))
                return word - low, found + 1

            _, found = lax.while_loop(lambda carry: carry[0] != 0, some, (bits_ref[w, row], found))
    rounds = lax.div(found + (UNROLL - 1), UNROLL)
    for j in range(UNROLL - 1):
        @pl.when(found + j < rounds * UNROLL)
        def _(j=j):
            note(found + j, n_slot * 1024)

    if n_begin:
        at = 0
        for begin_ref in begin_refs:
            acc[at:at + begin_ref.shape[0]] = begin_ref[...]
            at += begin_ref.shape[0]
        acc[at] = jnp.zeros_like(acc[at])
    else:
        acc[...] = jnp.zeros_like(acc)
    row_at = iota((COLS, COLS), 0)
    r1, c1 = iota((128, 128), 0), iota((128, 128), 1)
    both = ((0,), (0,))

    def step(i, carry):
        base = lax.rem(i, rings) * UNROLL
        for j in range(UNROLL):
            fetch(0, base + j).wait()
        for j in range(UNROLL):
            pair = pairs[i * UNROLL + j]
            slot = lax.shift_right_logical(pair, 10)
            rows = held[base + j]
            kept = jnp.where(row_at < 2 * cnt_ref[lax.bitwise_and(pair, 1023)], rows, jnp.zeros_like(rows))
            top = dot(kept[:, :128], rows, both)
            last = dot(kept[:, 128:], rows[:, 128:], both)
            acc[slot, 0:128] += jnp.where(r1 <= c1, top[:, :128], last)
            acc[slot, 128:256] += top[:, 128:]
            acc[slot, 256:264] += jnp.sum(jnp.where(r1 == c1, last, 0.0).reshape(16, 8, 128), axis=0)

        @pl.when(i + rings < rounds)
        def _():
            for j in range(UNROLL):
                fetch(lax.bitwise_and(pairs[(i + rings) * UNROLL + j], 1023), base + j).start()
        return carry

    lax.fori_loop(0, rounds, step, 0)
    at = 0
    for out, (distance, scenes) in zip(outs, groups):
        out[...] = acc[at:at + len(scenes)]
        at += len(scenes)


def partial_grams(me, bits, counts, tie_rows, groups, begin=()):
    smem = pl.BlockSpec(memory_space=pltpu.SMEM)
    vmem = pl.BlockSpec(memory_space=pltpu.VMEM)
    n_slot = sum(len(scenes) for _, scenes in groups)
    n_pairs = n_slot * tie_rows.shape[0] + UNROLL
    return pl.pallas_call(
        functools.partial(gram_kernel, groups, len(begin)),
        out_shape=[jax.ShapeDtypeStruct((len(scenes), PACK, 128), f32) for _, scenes in groups],
        in_specs=[smem, smem, smem, pl.BlockSpec(memory_space=pl.ANY)] + [vmem] * len(begin),
        out_specs=[vmem] * len(groups),
        scratch_shapes=[
            pltpu.VMEM((n_slot + 1, PACK, 128), f32),
            pltpu.VMEM((DEPTH, COLS, COLS), bf16),
            pltpu.SMEM(((n_pairs + 127) // 128 * 128,), jnp.int32),
            pltpu.SemaphoreType.DMA((DEPTH,)),
        ],
        compiler_params=pltpu.CompilerParams(vmem_limit_bytes=52 * 1024 * 1024),
        name="partial_grams",
    )(me, bits, counts, tie_rows, *begin)


def pattern_bits(pattern):
    n_scene, n_block = pattern.shape
    words = -(-n_block // WORD)
    block = jnp.arange(n_block, dtype=jnp.int32)
    bit = jnp.left_shift(1, block % WORD)
    weight = jnp.where(block[None, :] // WORD == jnp.arange(words, dtype=jnp.int32)[:, None], bit[None, :], 0)
    return jnp.sum(pattern[None, :, :] * weight[:, None, :], axis=2)


def ring(step, size):
    return [(i, (i + step) % size) for i in range(size)]


def share(value, axes, groups):
    sent = jnp.broadcast_to(value[None], (len(groups[0]),) + value.shape)
    return lax.all_to_all(sent, axes, 0, 0, axis_index_groups=groups, tiled=True)


def on_device(tie_rows, point_counts, pattern, sensitivity, damping, prior):
    owned = damping.shape[0]
    ways = lax.axis_size("tie")
    me = lax.axis_index("tie")
    me_word = me.reshape(1).astype(jnp.int32)
    near, far = (0, 1), (2, 3)
    up = functools.partial(lax.ppermute, axis_name="tie", perm=ring(1, ways))
    down = functools.partial(lax.ppermute, axis_name="tie", perm=ring(-1, ways))

    bits = pattern_bits(pattern)
    far_up, far_down = partial_grams(me_word, bits, point_counts, tie_rows, ((2, near), (2, far)))
    came_up, came_down = up(far_up), down(far_down)
    up_now, down_now = partial_grams(me_word, bits, point_counts, tie_rows, ((1, far), (3, near)))
    sens = lax.dynamic_slice_in_dim(sensitivity, me * owned, owned, 0)
    got_up, got_down = up(up_now), down(down_now)
    up_later, down_later = partial_grams(
        me_word, bits, point_counts, tie_rows, ((1, near), (3, far)), (came_up, came_down)
    )
    last_up, last_down = up(up_later), down(down_later)
    (own,) = partial_grams(me_word, bits, point_counts, tie_rows, ((0, near + far),))
    scene_rows, reduced = factor_scenes(own, (last_up, got_down), (got_up, last_down), sens, damping)

    n_scene = lax.axis_size("scene")
    plane = [[i for i in range(n_scene) if i % 2 == core] for core in range(2)]
    line = [list(range(ways))]
    chip = reduced + lax.ppermute(reduced, "scene", [(i, i ^ 1) for i in range(n_scene)])
    shares = share(chip, "scene", plane)
    total_parts = share(jnp.sum(shares, 0), "tie", line)
    global_factor = factor_total(total_parts, prior, float(owned * n_scene * ways))
    return (scene_rows, global_factor)


def solution(mesh):
    placed = (
        P("tie", None, None),
        P("tie"),
        P("scene", "tie"),
        P("scene", None, None),
        P(("scene", "tie")),
        P(),
    )
    return jax.shard_map(
        on_device,
        mesh=mesh,
        in_specs=placed,
        out_specs=(P(("scene", "tie"), None, None), P()),
        check_vma=False,
    )
```

```python
import functools

import jax
import jax.numpy as jnp
from jax import lax
from jax.experimental import pallas as pl
from jax.experimental.pallas import tpu as pltpu
from jax.sharding import PartitionSpec as P

SPLINE = 192
SHARED = 64
COLS = 256
PACK = 264
PANEL = 32
N_PANEL = SPLINE // PANEL
UNROLL = 8
DEPTH = 32
WORD = 24
f32 = jnp.float32
bf16 = jnp.bfloat16


def iota(shape, axis):
    return lax.broadcasted_iota(jnp.int32, shape, axis)


def split(x):
    high = x.astype(bf16)
    return high, (x - high.astype(f32)).astype(bf16)


def dot(a, b, contract=((1,), (0,))):
    return lax.dot_general(a, b, (contract, ((), ())), preferred_element_type=f32)


def dot3(a, b, contract=((1,), (0,))):
    a_high, a_low = split(a)
    b_high, b_low = split(b)
    return dot(a_high, b_high, contract) + (dot(a_low, b_high, contract) + dot(a_high, b_low, contract))


def outer_panel(left_high, left_low, right_high, right_low):
    left = jnp.concatenate([left_high, left_low, left_high, left_low], 0)
    right = jnp.concatenate([right_high, right_high, right_low, right_low], 0)
    return dot(left, right, ((0,), (0,)))


def invert_lower(packed):
    lane = iota((PANEL, 128), 1)
    group = lane - lax.rem(lane, PANEL)
    blocks = PANEL // 8
    sub = iota((8, 128), 0)
    columns = []
    for j in range(PANEL):
        wide = jnp.take_along_axis(packed, group + j, axis=1)
        columns.append([wide[8 * v:8 * v + 8] for v in range(blocks)])
    ident = (iota((PANEL, 128), 0) == lax.rem(lane, PANEL)).astype(f32)
    x = [ident[8 * v:8 * v + 8] for v in range(blocks)]

    def spread(block, at):
        return jnp.broadcast_to(block[at:at + 1], (8, 128))

    scales = [jnp.ones((8, 128), f32) for _ in range(blocks)]
    for k in range(PANEL):
        kv, ks = divmod(k, 8)
        pivot = spread(columns[k][kv], ks)
        inverse = 1.0 / pivot
        scales[kv] = jnp.where(sub == ks, lax.rsqrt(pivot), scales[kv])
        lower = [None] * kv + [columns[k][v] * inverse for v in range(kv, blocks)]
        for j in range(k + 1, PANEL):
            jv, js = divmod(j, 8)
            factor = spread(columns[k][jv], js)
            for v in range(jv, blocks):
                if j == k + 1:
                    columns[j][v] = columns[j][v] - (columns[k][v] * factor) * inverse
                else:
                    columns[j][v] = columns[j][v] - lower[v] * factor
        row = spread(x[kv], ks)
        for v in range(kv, blocks):
            below = jnp.where(sub > ks, lower[v], 0.0) if v == kv else lower[v]
            x[v] = x[v] - below * row
    x = [value * scale for value, scale in zip(x, scales)]
    return jnp.concatenate(x, 0)


def factor_kernel(damp_ref, own_ref, below_refs, above_refs, sens_ref, rows_ref, sum_ref, work):
    owned = rows_ref.shape[0]
    r1, c1 = iota((128, 128), 0), iota((128, 128), 1)
    tail_sum = jnp.zeros((SHARED, 128), f32)
    for s in range(owned):
        arrived, at = (below_refs, s) if s < owned // 2 else (above_refs, s - owned // 2)
        part = own_ref[s] + (arrived[0][at] + arrived[1][at])
        packed, side = part[:128], part[128:256]
        diagonal = jnp.sum(part[256:264], axis=0, keepdims=True)
        turned = packed.T
        first = jnp.where(r1 <= c1, packed, turned)
        last = jnp.where(r1 > c1, packed, jnp.where(r1 == c1, diagonal, turned))
        tail_sum = tail_sum + last[SHARED:]
        top = jnp.concatenate([
            jnp.concatenate([first, side], 1),
            jnp.concatenate([side.T[:SPLINE - 128], last[:SPLINE - 128]], 1),
        ], 0)
        sens = sens_ref[s]
        wide_sens = jnp.concatenate([sens, jnp.zeros((SPLINE, SHARED), bf16)], 1)
        high, low = split(top[:, :SPLINE])
        mixed = top + dot(high, wide_sens) + dot(low, wide_sens)
        high, low = split(mixed)
        both = ((0,), (0,))
        square = jnp.concatenate([wide_sens, jnp.zeros((COLS - SPLINE, COLS), bf16)], 0)
        pad = jnp.zeros((COLS - SPLINE, COLS), bf16)
        high, low = jnp.concatenate([high, pad], 0), jnp.concatenate([low, pad], 0)
        info = mixed + (dot(square, high, both) + dot(square, low, both))[:SPLINE]
        info = info + jnp.where(iota((SPLINE, COLS), 0) == iota((SPLINE, COLS), 1), damp_ref[s], 0.0)
        for p in range(N_PANEL):
            work[p, s * PANEL:(s + 1) * PANEL] = info[p * PANEL:(p + 1) * PANEL]

    lane = iota((PANEL, 128), 1)
    same = (r1 // PANEL) == (c1 // PANEL)
    row_in = lax.rem(iota((128, COLS), 0), PANEL)
    col_in = iota((128, COLS), 1)
    for p in range(N_PANEL):
        half, inner = divmod(p * PANEL, 128)
        current = work[p]
        packed = jnp.zeros((PANEL, 128), f32)
        for s in range(owned):
            piece = current[s * PANEL:(s + 1) * PANEL, half * 128:(half + 1) * 128]
            shift = (s * PANEL - inner) % 128
            if shift:
                piece = pltpu.roll(piece, shift, 1)
            packed = jnp.where(lane // PANEL == s, piece, packed)
        inverse = invert_lower(packed)
        spread = jnp.where(same, jnp.concatenate([inverse] * (128 // PANEL), 0), 0.0)
        rows = dot3(spread, current)
        rows = jnp.where(col_in >= row_in + p * PANEL, rows, 0.0)
        for s in range(owned):
            rows_ref[s, p * PANEL:(p + 1) * PANEL] = rows[s * PANEL:(s + 1) * PANEL]
        high, low = split(rows)
        start = ((p + 1) * PANEL) // 128 * 128
        if p + 1 < N_PANEL:
            for s in range(owned):
                at = slice(s * PANEL, (s + 1) * PANEL)
                update = outer_panel(high[at, start:], low[at, start:], high[at], low[at])
                for q in range(p + 1, N_PANEL):
                    work[q, at] = work[q, at] - update[q * PANEL - start:(q + 1) * PANEL - start]
        cross_high, cross_low = high[:, 128:], low[:, 128:]
        both = ((0,), (0,))
        outer = dot(cross_high, cross_high, both) + (dot(cross_high, cross_low, both) + dot(cross_low, cross_high, both))
        tail_sum = tail_sum - outer[SHARED:]
    whole = jnp.where(lane[:16] < SHARED, pltpu.roll(tail_sum[:16], SHARED, 1), tail_sum[16:PANEL])
    last = jnp.zeros((8, 128), f32)
    for i in range(4):
        piece = tail_sum[PANEL + 8 * i:PANEL + 8 * i + 8]
        if i < 3:
            piece = pltpu.roll(piece, PANEL * (i + 1), 1)
        last = jnp.where(lane[:8] // PANEL == i, piece, last)
    sum_ref[...] = jnp.concatenate([whole, last], 0)


def factor_scenes(own, below, above, sens, damping):
    owned = damping.shape[0]
    vmem = pl.BlockSpec(memory_space=pltpu.VMEM)

    def kernel(damp_ref, own_ref, b0, b1, a0, a1, *rest):
        factor_kernel(damp_ref, own_ref, (b0, b1), (a0, a1), *rest)

    return pl.pallas_call(
        kernel,
        out_shape=(
            jax.ShapeDtypeStruct((owned, SPLINE, COLS), f32),
            jax.ShapeDtypeStruct((24, 128), f32),
        ),
        in_specs=[pl.BlockSpec(memory_space=pltpu.SMEM)] + [vmem] * 6,
        out_specs=(vmem, vmem),
        scratch_shapes=[pltpu.VMEM((N_PANEL, owned * PANEL, COLS), f32)],
        compiler_params=pltpu.CompilerParams(vmem_limit_bytes=32 * 1024 * 1024),
        name="factor_scenes",
    )(damping, own, *below, *above, sens)


def total_kernel(count, prior_ref, parts_ref, out_ref):
    total = parts_ref[0]
    for i in range(1, parts_ref.shape[0]):
        total = total + parts_ref[i]
    total = total / count
    lane, row = iota((PANEL, 128), 1), iota((PANEL, 128), 0)
    prior = jnp.concatenate([prior_ref[...], prior_ref[...]], 1)
    last = [total[16:24] if i == 1 else pltpu.roll(total[16:24], (PANEL - PANEL * i) % 128, 1) for i in range(4)]
    bottom = jnp.concatenate(last, 0) + jnp.where(lane == row + PANEL, prior, 0.0)
    total = jnp.concatenate([total[:16], pltpu.roll(total[:16], SHARED, 1)], 0) + jnp.where(lane == row, prior, 0.0)
    first = jnp.where(lane < PANEL, invert_lower(total), 0.0)
    upper = dot3(first[:, :PANEL], total)
    upper = jnp.where((lane >= row) & (lane < SHARED), upper, 0.0)
    high, low = split(upper)
    bottom = jnp.where((lane >= PANEL) & (lane < SHARED), bottom - outer_panel(high, low, high, low)[PANEL:SHARED], 0.0)
    second = jnp.where(lane < PANEL, invert_lower(pltpu.roll(bottom, 128 - PANEL, 1)), 0.0)
    lower = dot3(second[:, :PANEL], bottom)
    lower = jnp.where(lane >= row + PANEL, lower, 0.0)
    out_ref[...] = jnp.concatenate([upper[:, :SHARED], lower[:, :SHARED]], 0)


def factor_total(parts, prior, count):
    vmem = pl.BlockSpec(memory_space=pltpu.VMEM)
    return pl.pallas_call(
        functools.partial(total_kernel, count),
        out_shape=jax.ShapeDtypeStruct((SHARED, SHARED), f32),
        in_specs=[vmem] * 2,
        out_specs=vmem,
        compiler_params=pltpu.CompilerParams(vmem_limit_bytes=8 * 1024 * 1024),
        name="factor_total",
    )(prior.reshape(1, SHARED), parts)


def gram_kernel(groups, n_begin, me_ref, bits_ref, cnt_ref, tie_ref, *rest):
    n_out = len(groups)
    begin_refs, rest = rest[:n_begin], rest[n_begin:]
    outs = rest[:n_out]
    acc, held, pairs, sems = rest[n_out:]
    slots = [(distance, scene) for distance, scenes in groups for scene in scenes]
    n_slot = len(slots)
    ways = 4
    rings = DEPTH // UNROLL

    def fetch(block, slot):
        return pltpu.make_async_copy(tie_ref.at[block], held.at[slot], sems.at[slot])

    def note(found, pair):
        pairs[found] = pair

        @pl.when(found < DEPTH)
        def _():
            fetch(lax.bitwise_and(pair, 1023), found).start()

    found = jnp.int32(0)
    for slot, (distance, scene) in enumerate(slots):
        row = lax.rem(me_ref[0] + distance, ways) * (bits_ref.shape[1] // ways) + scene
        for w in range(bits_ref.shape[0]):

            def some(carry, slot=slot, w=w):
                word, found = carry
                low = lax.bitwise_and(word, -word)
                note(found, slot * 1024 + w * WORD + 31 - lax.clz(low))
                return word - low, found + 1

            _, found = lax.while_loop(lambda carry: carry[0] != 0, some, (bits_ref[w, row], found))
    rounds = lax.div(found + (UNROLL - 1), UNROLL)
    for j in range(UNROLL - 1):
        @pl.when(found + j < rounds * UNROLL)
        def _(j=j):
            note(found + j, n_slot * 1024)

    if n_begin:
        at = 0
        for begin_ref in begin_refs:
            acc[at:at + begin_ref.shape[0]] = begin_ref[...]
            at += begin_ref.shape[0]
        acc[at] = jnp.zeros_like(acc[at])
    else:
        acc[...] = jnp.zeros_like(acc)
    row_at = iota((COLS, COLS), 0)
    r1, c1 = iota((128, 128), 0), iota((128, 128), 1)
    both = ((0,), (0,))

    def step(i, carry):
        base = lax.rem(i, rings) * UNROLL
        for j in range(UNROLL):
            fetch(0, base + j).wait()
        for j in range(UNROLL):
            pair = pairs[i * UNROLL + j]
            slot = lax.shift_right_logical(pair, 10)
            rows = held[base + j]
            kept = jnp.where(row_at < 2 * cnt_ref[lax.bitwise_and(pair, 1023)], rows, jnp.zeros_like(rows))
            top = dot(kept[:, :128], rows, both)
            last = dot(kept[:, 128:], rows[:, 128:], both)
            acc[slot, 0:128] += jnp.where(r1 <= c1, top[:, :128], last)
            acc[slot, 128:256] += top[:, 128:]
            acc[slot, 256:264] += jnp.sum(jnp.where(r1 == c1, last, 0.0).reshape(16, 8, 128), axis=0)

        @pl.when(i + rings < rounds)
        def _():
            for j in range(UNROLL):
                fetch(lax.bitwise_and(pairs[(i + rings) * UNROLL + j], 1023), base + j).start()
        return carry

    lax.fori_loop(0, rounds, step, 0)
    at = 0
    for out, (distance, scenes) in zip(outs, groups):
        out[...] = acc[at:at + len(scenes)]
        at += len(scenes)


def partial_grams(me, bits, counts, tie_rows, groups, begin=()):
    smem = pl.BlockSpec(memory_space=pltpu.SMEM)
    vmem = pl.BlockSpec(memory_space=pltpu.VMEM)
    n_slot = sum(len(scenes) for _, scenes in groups)
    n_pairs = n_slot * tie_rows.shape[0] + UNROLL
    return pl.pallas_call(
        functools.partial(gram_kernel, groups, len(begin)),
        out_shape=[jax.ShapeDtypeStruct((len(scenes), PACK, 128), f32) for _, scenes in groups],
        in_specs=[smem, smem, smem, pl.BlockSpec(memory_space=pl.ANY)] + [vmem] * len(begin),
        out_specs=[vmem] * len(groups),
        scratch_shapes=[
            pltpu.VMEM((n_slot + 1, PACK, 128), f32),
            pltpu.VMEM((DEPTH, COLS, COLS), bf16),
            pltpu.SMEM(((n_pairs + 127) // 128 * 128,), jnp.int32),
            pltpu.SemaphoreType.DMA((DEPTH,)),
        ],
        compiler_params=pltpu.CompilerParams(vmem_limit_bytes=52 * 1024 * 1024),
        name="partial_grams",
    )(me, bits, counts, tie_rows, *begin)


def pattern_bits(pattern):
    n_scene, n_block = pattern.shape
    words = -(-n_block // WORD)
    block = jnp.arange(n_block, dtype=jnp.int32)
    bit = jnp.left_shift(1, block % WORD)
    weight = jnp.where(block[None, :] // WORD == jnp.arange(words, dtype=jnp.int32)[:, None], bit[None, :], 0)
    return jnp.sum(pattern[None, :, :] * weight[:, None, :], axis=2)


def ring(step, size):
    return [(i, (i + step) % size) for i in range(size)]


def share(value, axes, groups):
    sent = jnp.broadcast_to(value[None], (len(groups[0]),) + value.shape)
    return lax.all_to_all(sent, axes, 0, 0, axis_index_groups=groups, tiled=True)


def on_device(tie_rows, point_counts, pattern, sensitivity, damping, prior):
    owned = damping.shape[0]
    ways = lax.axis_size("tie")
    me = lax.axis_index("tie")
    me_word = me.reshape(1).astype(jnp.int32)
    near, far = (0, 1), (2, 3)
    up = functools.partial(lax.ppermute, axis_name="tie", perm=ring(1, ways))
    down = functools.partial(lax.ppermute, axis_name="tie", perm=ring(-1, ways))

    bits = pattern_bits(pattern)
    far_up, far_down = partial_grams(me_word, bits, point_counts, tie_rows, ((2, near), (2, far)))
    came_up, came_down = up(far_up), down(far_down)
    up_now, down_now = partial_grams(me_word, bits, point_counts, tie_rows, ((1, far), (3, near)))
    sens = lax.dynamic_slice_in_dim(sensitivity, me * owned, owned, 0)
    got_up, got_down = up(up_now), down(down_now)
    up_later, down_later = partial_grams(
        me_word, bits, point_counts, tie_rows, ((1, near), (3, far)), (came_up, came_down)
    )
    last_up, last_down = up(up_later), down(down_later)
    (own,) = partial_grams(me_word, bits, point_counts, tie_rows, ((0, near + far),))
    scene_rows, reduced = factor_scenes(own, (last_up, got_down), (got_up, last_down), sens, damping)

    n_scene = lax.axis_size("scene")
    plane = [[i for i in range(n_scene) if i % 2 == core] for core in range(2)]
    line = [list(range(ways))]
    chip = reduced + lax.ppermute(reduced, "scene", [(i, i ^ 1) for i in range(n_scene)])
    shares = share(chip, "scene", plane)
    total_parts = share(jnp.sum(shares, 0), "tie", line)
    global_factor = factor_total(total_parts, prior, float(owned * n_scene * ways))
    return (scene_rows, global_factor)


def solution(mesh):
    placed = (
        P("tie", None, None),
        P("tie"),
        P("scene", "tie"),
        P("scene", None, None),
        P(("scene", "tie")),
        P(),
    )
    return jax.shard_map(
        on_device,
        mesh=mesh,
        in_specs=placed,
        out_specs=(P(("scene", "tie"), None, None), P()),
        check_vma=False,
    )
```
